32 devices in a mesh: stn: 8 (over y, x, core), chan: 4 (over z).
Axes of the slice: x: 2, y: 2, z: 4, core: 2. Of those that a mesh axis runs over, the one named last changes fastest.
Arguments:
- volts: bfloat16 [4, 2, 512, 18048], P('chan', None, 'stn'), may hold values from -6 to 6
- taps: float32 [16, 384], replicated, may hold values from -1.5 to 1.5
- survive: int32 [4, 8], replicated, may hold values from 0 to 383, as said below
- owner: int32 [4, 8], replicated, may hold values from 0 to 3, as said below
Outputs:
- visibilities: bfloat16 [4, 24, 2, 512, 512], P('chan', None, None, 'stn')
The draws below stay inside these ranges and needn't reach their ends.
Inputs may be any that keep to these rules, and one draw needn't show every extreme that they name: `survive`: each band lists 8 distinct fine channels. Within one band at most 6 channels share an owner, and in some band exactly 6 do; each owner holds at most 24 channels in all, and one owner holds exactly 24.
All inputs are finite; a program needn't handle non-finite values.
Results may differ from the reference program's by a relative error of at most 0.0076.
Values may be sent and summed in bfloat16 or wider, within the bound.
No kernel may reach another device: no remote copies, remote signals or barrier semaphores. Data moves between devices by JAX's collectives and lax.ppermute only.
A program may use at most 128 MiB of HBM per device.

```python
import math
import jax
import jax.numpy as jnp
from jax import lax

FINE = 384
TAPS = 16
NSPEC = 32
KEEP = 8
RCAP = 24
CAP = 6
COARSE = 4
NINP = 512
SAMP = 18048


def draw_survive(key, part):
    band_keys = jax.random.split(key, COARSE)
    return jax.vmap(lambda band_key: jax.random.permutation(band_key, FINE)[:KEEP])(band_keys).astype(jnp.int32)


def draw_owner(key, part):
    busy_key, shift_key, order_key = jax.random.split(key, 3)
    busy_owner = jax.random.randint(busy_key, (), 0, COARSE)
    busy_quota = RCAP // CAP
    busy_rest = RCAP % CAP
    window_width = min(busy_quota, COARSE)
    window_pick = jax.random.randint(shift_key, (), 0, window_width)
    rotation_offset = (busy_owner + COARSE // 2 - window_pick) % COARSE
    source_ids = jnp.arange(COARSE, dtype=jnp.int32)
    rotated = (source_ids - rotation_offset) % COARSE
    busy_count = jnp.where(rotated < busy_quota, CAP, jnp.where(rotated == busy_quota, busy_rest, 0))
    slot_ids = jnp.arange(KEEP, dtype=jnp.int32)
    leftover = slot_ids[None, :] - busy_count[:, None]
    other_owner = (busy_owner + 1 + (source_ids[:, None] + leftover + rotation_offset) % (COARSE - 1)) % COARSE
    base_owner = jnp.where(leftover < 0, busy_owner, other_owner)
    order_keys = jax.random.split(order_key, COARSE)
    orders = jax.vmap(lambda row_key: jax.random.permutation(row_key, KEEP))(order_keys)
    return jnp.take_along_axis(base_owner, orders, axis=1).astype(jnp.int32)


def level_of(key, shape, pieces, smallest, high):
    level = 1.0
    for position, shards_of in pieces:
        steps = jax.random.uniform(jax.random.fold_in(jax.random.fold_in(key, 6), position), (shards_of,), jnp.float32, smallest / len(pieces), high / len(pieces))
        level = level * jnp.repeat(jnp.exp(steps), shape[position] // shards_of).reshape((-1,) + (1,) * (len(shape) - 1 - position))
    return level


def bell_draw(stream_key, shape, scale, bound, cuts=(), kind=jnp.bfloat16):
    drawn = jax.random.normal(stream_key, shape, jnp.float32) * scale
    if len(cuts) > 0:
        drawn = level_of(stream_key, shape, cuts, -0.22, 0.18) * drawn
    return jnp.clip(drawn, min=-bound, max=bound).astype(kind)


def setup_inputs(seed: int = 0) -> dict:
    seeds = jax.random.split(jax.random.key(seed), 5)
    volts = bell_draw(seeds[0], (COARSE, 2, NINP, SAMP), 1.0, 6.0, ((0, 4), (2, 8)))
    taps = bell_draw(seeds[1], (TAPS, FINE), TAPS ** -0.5, 1.5, (), jnp.float32)
    survive = draw_survive(jax.random.fold_in(seeds[4], 71), 0)
    owner = draw_owner(jax.random.fold_in(seeds[4], 71), 0)
    return dict(volts=volts, taps=taps, survive=survive, owner=owner)


def fine_tables(chosen, fine_len):
    branch_ids = jnp.arange(fine_len, dtype=jnp.int32)
    phase_index = chosen[:, None] * branch_ids[None, :] % fine_len
    angles = phase_index.astype(jnp.float32) * (2.0 * math.pi / fine_len)
    factor = 1.0 / math.sqrt(fine_len)
    cosine = (jnp.cos(angles) * factor).astype(jnp.bfloat16)
    sine_table = (jnp.sin(angles) * factor).astype(jnp.bfloat16)
    return (cosine, sine_table)

def polyphase(signal, taps, spectra_count):
    accum = jnp.zeros((2, signal.shape[1], spectra_count, signal.shape[3]), jnp.float32)
    for tap_index in range(taps.shape[0]):
        accum = accum + taps[tap_index] * signal[:, :, tap_index:tap_index + spectra_count, :].astype(jnp.float32)
    return accum.astype(jnp.bfloat16)

def reference(volts, taps, survive, owner):

    def channelise(operands):
        band_volts, chosen = operands
        signal = band_volts.reshape(2, NINP, NSPEC + TAPS - 1, FINE)
        filtered = polyphase(signal, taps, NSPEC)
        cosine, sine_table = fine_tables(chosen, FINE)
        real_rows = filtered[0].reshape(NINP * NSPEC, FINE)
        imag_rows = filtered[1].reshape(NINP * NSPEC, FINE)
        real_part = jnp.dot(real_rows, cosine.T, preferred_element_type=jnp.float32) + jnp.dot(imag_rows, sine_table.T, preferred_element_type=jnp.float32)
        imag_part = jnp.dot(imag_rows, cosine.T, preferred_element_type=jnp.float32) - jnp.dot(real_rows, sine_table.T, preferred_element_type=jnp.float32)
        stacked = jnp.stack([real_part, imag_part]).astype(jnp.bfloat16).reshape(2, NINP, NSPEC, KEEP)
        return stacked.transpose(3, 2, 0, 1)
    spectra = lax.map(channelise, (volts, survive))
    flat = spectra.reshape(COARSE * KEEP, NSPEC, 2, NINP)

    def correlate(series):
        real_series = series[:, 0, :]
        imag_series = series[:, 1, :]
        real_part = jnp.dot(real_series.T, real_series, preferred_element_type=jnp.float32) + jnp.dot(imag_series.T, imag_series, preferred_element_type=jnp.float32)
        imag_part = jnp.dot(imag_series.T, real_series, preferred_element_type=jnp.float32) - jnp.dot(real_series.T, imag_series, preferred_element_type=jnp.float32)
        return (jnp.stack([real_part, imag_part]) / NSPEC).astype(jnp.bfloat16)
    grams = lax.map(correlate, flat)
    owners_flat = owner.reshape(-1)
    owner_hits = (owners_flat[:, None] == jnp.arange(COARSE, dtype=jnp.int32)[None, :]).astype(jnp.int32)
    owner_slot = lax.optimization_barrier(jnp.sum((jnp.cumsum(owner_hits, 0) - owner_hits) * owner_hits, 1))

    def place(slot_index):
        target = slot_index // RCAP
        within = slot_index % RCAP
        chosen_mask = ((owners_flat == target) & (owner_slot == within)).astype(jnp.int32)
        source = jnp.argmax(chosen_mask).astype(jnp.int32)
        present = jnp.max(chosen_mask)
        picked = lax.dynamic_index_in_dim(grams, source, 0, keepdims=False)
        return jnp.where(present > 0, picked, jnp.zeros_like(picked))
    visibilities = lax.map(place, jnp.arange(COARSE * RCAP, dtype=jnp.int32))
    return visibilities.reshape(COARSE, RCAP, 2, NINP, NINP)
```

```python
import functools
import math

import jax
import jax.numpy as jnp
from jax import lax
from jax.experimental import pallas as pl
from jax.experimental.pallas import tpu as pltpu
from jax.sharding import PartitionSpec as P

RCAP = 24
LANES = 128
GROUP = 4
VMEM_LIMIT = 48 << 20


def swapped(x, axis, mask):
    peers = lax.axis_size(axis)
    return lax.ppermute(x, axis, [(i, i ^ mask) for i in range(peers)])


def front_kernel(chan_count, slot_cap, survive_ref, owner_ref, taps_ref, volts_ref, *rest):
    outs = rest[:chan_count]
    volts, table, even, odd, spectra, stage, in_sems, out_sems = rest[chan_count:]
    taps_count, fine_len = taps_ref.shape
    inputs, samples = volts_ref.shape[2:]
    keep = survive_ref.shape[1]
    blocks = samples // fine_len
    times = blocks - taps_count + 1
    pack = max(1, LANES // inputs)
    rows = times // pack
    band = lax.axis_index("chan")

    groups = []
    for first in range(0, blocks, GROUP):
        count = min(GROUP, blocks - first)
        lanes = pl.ds(first * fine_len, count * fine_len)
        copy = pltpu.make_async_copy(
            volts_ref.at[0, :, :, lanes], volts.at[:, :, lanes], in_sems.at[first // GROUP]
        )
        copy.start()
        groups.append((first, count, copy))

    row_ids = lax.broadcasted_iota(jnp.int32, (keep, fine_len), 0)
    branch_ids = lax.broadcasted_iota(jnp.int32, (keep, fine_len), 1)
    chosen = jnp.zeros((keep, fine_len), jnp.int32)
    for c in range(keep):
        chosen = jnp.where(row_ids == c, survive_ref[band, c], chosen)
    angles = (chosen * branch_ids % fine_len).astype(jnp.float32) * (2.0 * math.pi / fine_len)
    factor = 1.0 / math.sqrt(fine_len)
    cosine = (jnp.cos(angles) * factor).astype(jnp.bfloat16).astype(jnp.float32)
    sine = (jnp.sin(angles) * factor).astype(jnp.bfloat16).astype(jnp.float32)
    real_row = jnp.concatenate([cosine, sine], 1)
    imag_row = jnp.concatenate([-sine, cosine], 1)
    both = jnp.concatenate([real_row, imag_row], 0)
    for p in range(taps_count):
        tap = taps_ref[p : p + 1, :]
        table[p * 2 * keep : (p + 1) * 2 * keep, :] = (
            both * jnp.concatenate([tap, tap], 1)
        ).astype(jnp.bfloat16)

    stage[...] = jnp.zeros_like(stage)
    even[...] = jnp.zeros_like(even)
    odd[...] = jnp.zeros_like(odd)
    for first, count, copy in groups:
        copy.wait()
        parts = []
        for s in range(first, first + count):
            lanes = slice(s * fine_len, (s + 1) * fine_len)
            parts.append(jnp.concatenate([volts[0, :, lanes], volts[1, :, lanes]], 1))
        if (count * inputs) % LANES:
            parts.append(parts[-1])
        signal = jnp.concatenate(parts, 0)
        products = lax.dot_general(
            table[...], signal, (((1,), (1,)), ((), ())), preferred_element_type=jnp.float32
        )
        for u in range(first // pack, (first + len(parts)) // pack):
            lanes = slice((u - first // pack) * LANES, (u - first // pack + 1) * LANES)
            for p in range(taps_count):
                term = products[p * 2 * keep : (p + 1) * 2 * keep, lanes]
                v = u - p // pack
                if p % pack == 0:
                    if 0 <= v < rows:
                        even[v] += term
                elif 0 <= v <= rows:
                    odd[v] += term

    first_half = lax.broadcasted_iota(jnp.int32, (2 * keep, LANES), 1) < LANES // 2
    for v in range(rows):
        total = even[v]
        if pack == 2:
            late = jnp.where(first_half, odd[v + 1], odd[v])
            total = total + pltpu.roll(late, LANES // 2, 1)
        spectra[v * 2 * keep : (v + 1) * 2 * keep, :] = total

    for c in range(keep):
        owner = owner_ref[band, c]
        rank = jnp.int32(0)
        for earlier in range(c):
            rank += (owner_ref[band, earlier] == owner).astype(jnp.int32)
        piece = owner ^ band
        for part in range(2):
            line = spectra[pl.ds(part * keep + c, rows, stride=2 * keep), :]
            stage[piece, rank, part * rows : (part + 1) * rows, :] = line.astype(jnp.bfloat16)

    copies = []
    for k in range(chan_count):
        copy = pltpu.make_async_copy(stage.at[k], outs[k], out_sems.at[k])
        copy.start()
        copies.append(copy)
    for copy in copies:
        copy.wait()


def back_kernel(stn_count, chan_count, slot_cap, times, owner_ref, near_ref, far_ref, out_ref, *rest):
    result, zeros, sems = rest
    keep = owner_ref.shape[1]
    inputs = out_ref.shape[2]
    slots = chan_count * slot_cap
    band = lax.axis_index("chan")
    stn = lax.axis_index("stn")
    chip = stn // 2
    core = stn % 2
    pack = max(1, LANES // inputs)
    rows = times // pack

    held = []
    for b in range(chan_count):
        count = jnp.int32(0)
        for c in range(keep):
            count += (owner_ref[b, c] == band).astype(jnp.int32)
        held.append(count)
    total = functools.reduce(lambda x, y: x + y, held)

    zeros[...] = jnp.zeros_like(zeros)
    for slot in range(RCAP):

        @pl.when(slot >= total)
        def _():
            pltpu.make_async_copy(zeros, out_ref.at[slot], sems.at[slot]).start()

    def halves(x, y):
        if pack == 1:
            return jnp.concatenate([x, y], 1)
        return jnp.concatenate(
            [
                jnp.concatenate([x[:, :inputs], y[:, :inputs]], 1),
                jnp.concatenate([x[:, inputs:], y[:, inputs:]], 1),
            ],
            0,
        )

    for k in range(chan_count):
        source = band ^ k
        base = jnp.int32(0)
        count = jnp.int32(0)
        for b in range(chan_count):
            base += jnp.where(b < source, held[b], 0)
            count += jnp.where(b == source, held[b], 0)
        for j in range(slot_cap):
            slot = k * slot_cap + j
            mine = near_ref[slot]
            turned = jnp.concatenate([mine[rows:], -mine[:rows]], 0)
            left = halves(mine, turned)
            right = []
            for other in range(stn_count // 2):
                index = (chip ^ other) * slots + slot
                x = near_ref[index]
                y = far_ref[index]
                right.append(halves(jnp.where(core == 0, x, y), jnp.where(core == 0, y, x)))
            products = lax.dot_general(
                left,
                jnp.concatenate(right, 1),
                (((0,), (0,)), ((), ())),
                preferred_element_type=jnp.float32,
            )
            products = (products * (1.0 / times)).astype(jnp.bfloat16)
            result[slot, 0] = products[:inputs]
            result[slot, 1] = products[inputs:]
        for j in range(slot_cap):

            @pl.when(j < count)
            def _():
                pltpu.make_async_copy(
                    result.at[k * slot_cap + j], out_ref.at[base + j], sems.at[base + j]
                ).start()

    for slot in range(RCAP):
        pltpu.make_async_copy(zeros, out_ref.at[slot], sems.at[slot]).wait()


def per_device(volts, taps, survive, owner):
    chan_count = lax.axis_size("chan")
    stn_count = lax.axis_size("stn")
    inputs, samples = volts.shape[2:]
    taps_count, fine_len = taps.shape
    keep = survive.shape[1]
    blocks = samples // fine_len
    times = blocks - taps_count + 1
    slot_cap = max(2, (RCAP + chan_count - 1) // chan_count)
    pack = max(1, LANES // inputs)
    rows = times // pack
    smem = pl.BlockSpec(memory_space=pltpu.SMEM)
    vmem = pl.BlockSpec(memory_space=pltpu.VMEM)
    anywhere = pl.BlockSpec(memory_space=pl.ANY)

    block = (slot_cap, 2 * rows, pack * inputs)
    pieces = pl.pallas_call(
        functools.partial(front_kernel, chan_count, slot_cap),
        out_shape=[jax.ShapeDtypeStruct(block, jnp.bfloat16)] * chan_count,
        in_specs=[smem, smem, vmem, anywhere],
        out_specs=[anywhere] * chan_count,
        scratch_shapes=[
            pltpu.VMEM((2, inputs, samples), jnp.bfloat16),
            pltpu.VMEM((taps_count * 2 * keep, 2 * fine_len), jnp.bfloat16),
            pltpu.VMEM((rows, 2 * keep, LANES), jnp.float32),
            pltpu.VMEM((rows + 1, 2 * keep, LANES), jnp.float32),
            pltpu.VMEM((rows * 2 * keep, LANES), jnp.float32),
            pltpu.VMEM((chan_count,) + block, jnp.bfloat16),
            pltpu.SemaphoreType.DMA((-(-blocks // GROUP),)),
            pltpu.SemaphoreType.DMA((chan_count,)),
        ],
        compiler_params=pltpu.CompilerParams(vmem_limit_bytes=VMEM_LIMIT),
    )(survive, owner, taps, volts)

    held = jnp.concatenate(
        [pieces[0]] + [swapped(pieces[k], "chan", k) for k in range(1, chan_count)], 0
    )
    near = jnp.concatenate([held] + [swapped(held, "stn", m) for m in range(2, stn_count, 2)], 0)
    far = swapped(near, "stn", 1)

    out_shape = (RCAP, 2, inputs, stn_count * inputs)
    visibilities = pl.pallas_call(
        functools.partial(back_kernel, stn_count, chan_count, slot_cap, times),
        out_shape=jax.ShapeDtypeStruct(out_shape, jnp.bfloat16),
        in_specs=[smem, vmem, vmem],
        out_specs=anywhere,
        scratch_shapes=[
            pltpu.VMEM((chan_count * slot_cap,) + out_shape[1:], jnp.bfloat16),
            pltpu.VMEM(out_shape[1:], jnp.bfloat16),
            pltpu.SemaphoreType.DMA((RCAP,)),
        ],
        compiler_params=pltpu.CompilerParams(vmem_limit_bytes=VMEM_LIMIT),
    )(owner, near, far)
    return visibilities[None]


def solution(mesh):
    return jax.shard_map(
        per_device,
        mesh=mesh,
        in_specs=(P("chan", None, "stn", None), P(), P(), P()),
        out_specs=P("chan", None, None, "stn", None),
        check_vma=False,
    )
```

```python
import functools
import math

import jax
import jax.numpy as jnp
from jax import lax
from jax.experimental import pallas as pl
from jax.experimental.pallas import tpu as pltpu
from jax.sharding import PartitionSpec as P

RCAP = 24
LANES = 128
GROUPS = (24, 23)
FRONT_VMEM = 62 << 20
BACK_VMEM = 16 << 20


def swapped(x, axis, mask):
    peers = lax.axis_size(axis)
    return lax.ppermute(x, axis, [(i, i ^ mask) for i in range(peers)])


def group_sizes(blocks):
    groups, first = [], 0
    while first < blocks:
        count = min(GROUPS[min(len(groups), len(GROUPS) - 1)], blocks - first)
        groups.append((first, count))
        first += count
    return groups


def front_kernel(chan_count, slot_cap, survive_any, owner_any, taps_any, volts_ref, *rest):
    outs = rest[:chan_count]
    volts, survive_ref, owner_ref, taps_ref, table, products, spectra, stage = rest[
        chan_count:-3
    ]
    in_sems, small_sems, out_sems = rest[-3:]
    taps_count, fine_len = taps_ref.shape
    inputs, samples = volts_ref.shape[2:]
    keep = survive_ref.shape[1]
    blocks = samples // fine_len
    times = blocks - taps_count + 1
    pack = max(1, LANES // inputs)
    rows = times // pack
    band = lax.axis_index("chan")

    small = []
    for n, (source, target) in enumerate(
        ((survive_any, survive_ref), (taps_any, taps_ref), (owner_any, owner_ref))
    ):
        copy = pltpu.make_async_copy(source, target, small_sems.at[n])
        copy.start()
        small.append(copy)
    groups = []
    for first, count in group_sizes(blocks):
        lanes = pl.ds(first * fine_len, count * fine_len)
        copy = pltpu.make_async_copy(
            volts_ref.at[0, :, :, lanes], volts.at[:, :, lanes], in_sems.at[len(groups)]
        )
        copy.start()
        groups.append((first, count, copy))

    small[0].wait()
    row_ids = lax.broadcasted_iota(jnp.int32, (keep, fine_len), 0)
    branch_ids = lax.broadcasted_iota(jnp.int32, (keep, fine_len), 1)
    chosen = jnp.zeros((keep, fine_len), jnp.int32)
    for c in range(keep):
        chosen = jnp.where(row_ids == c, survive_ref[band, c], chosen)
    angles = (chosen * branch_ids % fine_len).astype(jnp.float32) * (2.0 * math.pi / fine_len)
    factor = 1.0 / math.sqrt(fine_len)
    cosine = (jnp.cos(angles) * factor).astype(jnp.bfloat16).astype(jnp.float32)
    sine = (jnp.sin(angles) * factor).astype(jnp.bfloat16).astype(jnp.float32)
    real_row = jnp.concatenate([cosine, sine], 1)
    imag_row = jnp.concatenate([-sine, cosine], 1)
    both = jnp.concatenate([real_row, imag_row], 0)
    small[1].wait()
    for p in range(taps_count):
        tap = taps_ref[p : p + 1, :]
        table[p * 2 * keep : (p + 1) * 2 * keep, :] = (
            both * jnp.concatenate([tap, tap], 1)
        ).astype(jnp.bfloat16)

    stage[...] = jnp.zeros_like(stage)
    first_half = lax.broadcasted_iota(jnp.int32, (2 * keep, LANES), 1) < LANES // 2

    def finish(v):
        sums = [None] * (2 * pack - 1)
        for p in range(taps_count):
            for late in range(1 if p % pack == 0 else 2):
                u = v + p // pack + late
                which = 0 if p % pack == 0 else 1 + late
                term = products[p * 2 * keep : (p + 1) * 2 * keep, u * LANES : (u + 1) * LANES]
                sums[which] = term if sums[which] is None else sums[which] + term
        total = sums[0]
        if pack == 2:
            total = total + pltpu.roll(jnp.where(first_half, sums[2], sums[1]), LANES // 2, 1)
        spectra[v * 2 * keep : (v + 1) * 2 * keep, :] = total

    done = 0
    ready = 0
    for first, count, copy in groups:
        copy.wait()
        parts = []
        for s in range(first, first + count):
            lanes = slice(s * fine_len, (s + 1) * fine_len)
            parts.append(jnp.concatenate([volts[0, :, lanes], volts[1, :, lanes]], 1))
        if (count * inputs) % LANES:
            parts.append(parts[-1])
        end = first + len(parts)
        products[:, first * inputs : end * inputs] = lax.dot_general(
            table[...],
            jnp.concatenate(parts, 0),
            (((1,), (1,)), ((), ())),
            preferred_element_type=jnp.float32,
        )
        while done < ready:
            finish(done)
            done += 1
        ready = min(rows, max(0, end // pack - (taps_count - 1 + pack - 1) // pack))
    while done < rows:
        finish(done)
        done += 1

    small[2].wait()
    for c in range(keep):
        owner = owner_ref[band, c]
        rank = jnp.int32(0)
        for earlier in range(c):
            rank += (owner_ref[band, earlier] == owner).astype(jnp.int32)
        piece = owner ^ band
        for part in range(2):
            line = spectra[pl.ds(part * keep + c, rows, stride=2 * keep), :]
            stage[piece, rank, part * rows : (part + 1) * rows, :] = line.astype(jnp.bfloat16)

    copies = []
    for k in range(chan_count):
        copy = pltpu.make_async_copy(stage.at[k], outs[k], out_sems.at[k])
        copy.start()
        copies.append(copy)
    for copy in copies:
        copy.wait()


def back_kernel(others, stn_count, slot_cap, times, aliased, owner_any, held_ref, *rest):
    near_refs = rest[: len(others)]
    far_refs = rest[len(others) : 2 * len(others)]
    out_ref, result, zeros, owner_ref, owner_sem, out_sem = rest[2 * len(others) + aliased :]
    bands, keep = owner_ref.shape
    inputs = out_ref.shape[2]
    width = 2 * inputs
    band = lax.axis_index("chan")
    stn = lax.axis_index("stn")
    chip = stn // 2
    core = stn % 2
    pack = max(1, LANES // inputs)
    rows = times // pack
    owner_copy = pltpu.make_async_copy(owner_any, owner_ref, owner_sem)
    owner_copy.start()
    zeros[...] = jnp.zeros_like(zeros)

    def halves(x, y):
        if pack == 1:
            return jnp.concatenate([x, y], 1)
        return jnp.concatenate(
            [
                jnp.concatenate([x[:, :inputs], y[:, :inputs]], 1),
                jnp.concatenate([x[:, inputs:], y[:, inputs:]], 1),
            ],
            0,
        )

    def correlate(slot):
        mine = held_ref[slot]
        left = halves(mine, jnp.concatenate([mine[rows:], -mine[:rows]], 0))
        right = []
        for near_ref, far_ref in zip(near_refs, far_refs):
            x = near_ref[slot]
            y = far_ref[slot]
            right.append(halves(jnp.where(core == 0, x, y), jnp.where(core == 0, y, x)))
        products = lax.dot_general(
            left,
            jnp.concatenate(right, 1),
            (((0,), (0,)), ((), ())),
            preferred_element_type=jnp.float32,
        )
        products = (products * (1.0 / times)).astype(jnp.bfloat16)
        for n in range(len(others)):
            lanes = slice(n * width, (n + 1) * width)
            result[slot, n, 0] = products[:inputs, lanes]
            result[slot, n, 1] = products[inputs:, lanes]

    def store(source, n, slot):
        column = pl.multiple_of((chip ^ others[n]) * width, LANES)
        return pltpu.make_async_copy(
            source, out_ref.at[slot, :, :, pl.ds(column, width)], out_sem.at[slot, n]
        )

    for j in range(slot_cap):
        correlate(j)

    owner_copy.wait()
    held = []
    for b in range(bands):
        count = jnp.int32(0)
        for c in range(keep):
            count += (owner_ref[b, c] == band).astype(jnp.int32)
        held.append(count)
    total = functools.reduce(lambda x, y: x + y, held)

    for k in range(bands):
        if k > 0:
            for j in range(slot_cap):
                correlate(k * slot_cap + j)
        source = band ^ k
        base = jnp.int32(0)
        count = jnp.int32(0)
        for b in range(bands):
            base += jnp.where(b < source, held[b], 0)
            count += jnp.where(b == source, held[b], 0)
        for j in range(slot_cap):

            @pl.when(j < count)
            def _():
                for n in range(len(others)):
                    store(result.at[k * slot_cap + j, n], n, base + j).start()

    for slot in range(RCAP):

        @pl.when(slot >= total)
        def _():
            for n in range(len(others)):
                store(zeros, n, slot).start()

    for slot in range(RCAP):
        for n in range(len(others)):
            store(zeros, n, slot).wait()


def per_device(volts, taps, survive, owner):
    chan_count = lax.axis_size("chan")
    stn_count = lax.axis_size("stn")
    inputs, samples = volts.shape[2:]
    taps_count, fine_len = taps.shape
    keep = survive.shape[1]
    blocks = samples // fine_len
    times = blocks - taps_count + 1
    slot_cap = max(2, (RCAP + chan_count - 1) // chan_count)
    pack = max(1, LANES // inputs)
    rows = times // pack
    smem = pl.BlockSpec(memory_space=pltpu.SMEM)
    vmem = pl.BlockSpec(memory_space=pltpu.VMEM)
    anywhere = pl.BlockSpec(memory_space=pl.ANY)

    block = (slot_cap, 2 * rows, pack * inputs)
    pieces = pl.pallas_call(
        functools.partial(front_kernel, chan_count, slot_cap),
        out_shape=[jax.ShapeDtypeStruct(block, jnp.bfloat16)] * chan_count,
        in_specs=[anywhere] * 4,
        out_specs=[anywhere] * chan_count,
        scratch_shapes=[
            pltpu.VMEM((2, inputs, samples), jnp.bfloat16),
            pltpu.SMEM(survive.shape, jnp.int32),
            pltpu.SMEM(owner.shape, jnp.int32),
            pltpu.VMEM(taps.shape, jnp.float32),
            pltpu.VMEM((taps_count * 2 * keep, 2 * fine_len), jnp.bfloat16),
            pltpu.VMEM((taps_count * 2 * keep, -(-blocks // pack) * pack * inputs), jnp.float32),
            pltpu.VMEM((rows * 2 * keep, LANES), jnp.float32),
            pltpu.VMEM((chan_count,) + block, jnp.bfloat16),
            pltpu.SemaphoreType.DMA((len(group_sizes(blocks)),)),
            pltpu.SemaphoreType.DMA((3,)),
            pltpu.SemaphoreType.DMA((chan_count,)),
        ],
        compiler_params=pltpu.CompilerParams(vmem_limit_bytes=FRONT_VMEM),
    )(survive, owner, taps, volts)

    held = jnp.concatenate(
        [pieces[0]] + [swapped(pieces[k], "chan", k) for k in range(1, chan_count)], 0
    )
    chips = list(range(stn_count // 2))
    near = [held] + [swapped(held, "stn", 2 * n) for n in chips[1:]]
    far = [swapped(x, "stn", 1) for x in near[:-1]]

    out_shape = (RCAP, 2, inputs, stn_count * inputs)

    def back(others, previous):
        blocks_in = [near[n] for n in others] + [far[n] for n in others]
        aliased = 0 if previous is None else 1
        slots = held.shape[0]
        return pl.pallas_call(
            functools.partial(back_kernel, others, stn_count, slot_cap, times, aliased),
            out_shape=jax.ShapeDtypeStruct(out_shape, jnp.bfloat16),
            in_specs=[anywhere] + [vmem] * (1 + len(blocks_in)) + [anywhere] * aliased,
            out_specs=anywhere,
            input_output_aliases={2 + len(blocks_in): 0} if aliased else {},
            scratch_shapes=[
                pltpu.VMEM((slots, len(others), 2, inputs, 2 * inputs), jnp.bfloat16),
                pltpu.VMEM((2, inputs, 2 * inputs), jnp.bfloat16),
                pltpu.SMEM(owner.shape, jnp.int32),
                pltpu.SemaphoreType.DMA(()),
                pltpu.SemaphoreType.DMA((RCAP, len(others))),
            ],
            compiler_params=pltpu.CompilerParams(vmem_limit_bytes=BACK_VMEM),
            cost_estimate=pl.CostEstimate(flops=1000, bytes_accessed=1000, transcendentals=0),
        )(owner, held, *blocks_in, *([previous] if aliased else []))

    visibilities = back(chips[:1], None)
    near[-1], visibilities = lax.optimization_barrier((near[-1], visibilities))
    far.append(swapped(near[-1], "stn", 1))
    visibilities = back(chips[1:-1], visibilities)
    visibilities = back(chips[-1:], visibilities)
    return visibilities[None]


def solution(mesh):
    return jax.shard_map(
        per_device,
        mesh=mesh,
        in_specs=(P("chan", None, "stn", None), P(), P(), P()),
        out_specs=P("chan", None, None, "stn", None),
        check_vma=False,
    )
```

```python
import functools
import math

import jax
import jax.numpy as jnp
from jax import lax
from jax.experimental import pallas as pl
from jax.experimental.pallas import tpu as pltpu
from jax.sharding import PartitionSpec as P

RCAP = 24
BATCH = 6
LANES = 128
GROUPS = (24, 23)
FRONT_VMEM = 62 << 20
BACK_VMEM = 16 << 20


def swapped(x, axis, mask):
    peers = lax.axis_size(axis)
    return lax.ppermute(x, axis, [(i, i ^ mask) for i in range(peers)])


def group_sizes(blocks):
    groups, first = [], 0
    while first < blocks:
        count = min(GROUPS[min(len(groups), len(GROUPS) - 1)], blocks - first)
        groups.append((first, count))
        first += count
    return groups


def front_kernel(chan_count, slot_cap, survive_any, owner_any, taps_any, volts_ref, *rest):
    outs = rest[:chan_count]
    volts, survive_ref, owner_ref, taps_ref = rest[chan_count:-7]
    table, products, spectra, stage, in_sems, small_sems, out_sems = rest[-7:]
    taps_count, fine_len = taps_ref.shape
    inputs, samples = volts_ref.shape[2:]
    keep = survive_ref.shape[1]
    blocks = samples // fine_len
    times = blocks - taps_count + 1
    pack = max(1, LANES // inputs)
    lines = times // pack
    band = lax.axis_index("chan")
    core = lax.axis_index("stn") % 2

    small = []
    for n, (source, target) in enumerate(
        ((survive_any, survive_ref), (taps_any, taps_ref), (owner_any, owner_ref))
    ):
        copy = pltpu.make_async_copy(source, target, small_sems.at[n])
        copy.start()
        small.append(copy)
    groups = []
    for first, count in group_sizes(blocks):
        lanes = pl.ds(first * fine_len, count * fine_len)
        copy = pltpu.make_async_copy(
            volts_ref.at[0, :, :, lanes], volts.at[:, :, lanes], in_sems.at[len(groups)]
        )
        copy.start()
        groups.append((first, count, copy))

    small[0].wait()
    row_ids = lax.broadcasted_iota(jnp.int32, (keep, fine_len), 0)
    branch_ids = lax.broadcasted_iota(jnp.int32, (keep, fine_len), 1)
    chosen = jnp.zeros((keep, fine_len), jnp.int32)
    for c in range(keep):
        chosen = jnp.where(row_ids == c, survive_ref[band, c], chosen)
    angles = (chosen * branch_ids % fine_len).astype(jnp.float32) * (2.0 * math.pi / fine_len)
    factor = 1.0 / math.sqrt(fine_len)
    cosine = (jnp.cos(angles) * factor).astype(jnp.bfloat16).astype(jnp.float32)
    sine = (jnp.sin(angles) * factor).astype(jnp.bfloat16).astype(jnp.float32)
    real_row = jnp.concatenate([cosine, sine], 1)
    imag_row = jnp.concatenate([-sine, cosine], 1)
    both = jnp.concatenate([real_row, imag_row], 0)
    small[1].wait()
    for p in range(taps_count):
        tap = taps_ref[p : p + 1, :]
        table[p * 2 * keep : (p + 1) * 2 * keep, :] = (
            both * jnp.concatenate([tap, tap], 1)
        ).astype(jnp.bfloat16)

    stage[...] = jnp.zeros_like(stage)
    first_half = lax.broadcasted_iota(jnp.int32, (2 * keep, LANES), 1) < LANES // 2

    def finish(v):
        sums = [None] * (2 * pack - 1)
        for p in range(taps_count):
            for late in range(1 if p % pack == 0 else 2):
                u = v + p // pack + late
                which = 0 if p % pack == 0 else 1 + late
                term = products[p * 2 * keep : (p + 1) * 2 * keep, u * LANES : (u + 1) * LANES]
                sums[which] = term if sums[which] is None else sums[which] + term
        total = sums[0]
        if pack == 2:
            late = jnp.where(first_half, sums[2], sums[1])
            total = jnp.where(core == 0, total, late) + pltpu.roll(
                jnp.where(core == 0, late, total), LANES // 2, 1
            )
        spectra[v * 2 * keep : (v + 1) * 2 * keep, :] = total

    done = 0
    ready = 0
    for first, count, copy in groups:
        copy.wait()
        parts = []
        for s in range(first, first + count):
            lanes = slice(s * fine_len, (s + 1) * fine_len)
            parts.append(jnp.concatenate([volts[0, :, lanes], volts[1, :, lanes]], 1))
        if (count * inputs) % LANES:
            parts.append(parts[-1])
        end = first + len(parts)
        products[:, first * inputs : end * inputs] = lax.dot_general(
            table[...],
            jnp.concatenate(parts, 0),
            (((1,), (1,)), ((), ())),
            preferred_element_type=jnp.float32,
        )
        while done < ready:
            finish(done)
            done += 1
        ready = min(lines, max(0, end // pack - (taps_count - 1 + pack - 1) // pack))
    while done < lines:
        finish(done)
        done += 1

    small[2].wait()
    for c in range(keep):
        owner = owner_ref[band, c]
        rank = jnp.int32(0)
        for earlier in range(c):
            rank += (owner_ref[band, earlier] == owner).astype(jnp.int32)
        piece = owner ^ band
        for part in range(2):
            line = spectra[pl.ds(part * keep + c, lines, stride=2 * keep), :]
            stage[piece, rank, part * lines : (part + 1) * lines, :] = line.astype(jnp.bfloat16)

    copies = []
    for k in range(chan_count):
        copy = pltpu.make_async_copy(stage.at[k], outs[k], out_sems.at[k])
        copy.start()
        copies.append(copy)
    for copy in copies:
        copy.wait()


def back_kernel(sequences, order, slot_cap, times, owner_any, *rest):
    chips = len(sequences)
    near = rest[:chips]
    far = [rest[chips + sequences.index((m, n))] for n, m in sequences]
    out_ref, result, zeros, owner_ref, owner_sem, sems, zero_sems = rest[2 * chips :]
    bands, keep = owner_ref.shape
    slots = near[0].shape[0]
    inputs = out_ref.shape[2]
    band = lax.axis_index("chan")
    stn = lax.axis_index("stn")
    chip = stn // 2
    core = stn % 2
    pack = max(1, LANES // inputs)
    lines = times // pack
    owner_copy = pltpu.make_async_copy(owner_any, owner_ref, owner_sem)
    owner_copy.start()
    zeros[...] = jnp.zeros_like(zeros)

    lane = lax.broadcasted_iota(jnp.int32, (2 * lines, LANES), 1)
    low = lane < LANES // 2
    first = (lane // (LANES // 2)) == core

    def turn(x):
        return jnp.concatenate([x[:, LANES // 2 :], x[:, : LANES // 2]], 1)

    def correlate(slot):
        mine = near[0][slot]
        turned = jnp.concatenate([mine[lines:], -mine[:lines]], 0)
        if pack == 1:
            left = jnp.concatenate([mine, turned], 1)
        else:
            ahead = jnp.where(low, mine, turn(turned))
            behind = jnp.where(low, turn(mine), turned)
            left = jnp.concatenate(
                [jnp.where(core == 0, ahead, behind), jnp.where(core == 0, behind, ahead)], 0
            )
        right = []
        for near_ref, far_ref in zip(near, far):
            x = near_ref[slot]
            y = far_ref[slot]
            if pack == 1:
                right.append(
                    jnp.concatenate([jnp.where(core == 0, x, y), jnp.where(core == 0, y, x)], 1)
                )
            else:
                right.append(
                    jnp.concatenate([jnp.where(first, x, y), turn(jnp.where(first, y, x))], 0)
                )
        products = lax.dot_general(
            left,
            jnp.concatenate(right, 1),
            (((0,), (0,)), ((), ())),
            preferred_element_type=jnp.float32,
        )
        products = (products * (1.0 / times)).astype(jnp.bfloat16)
        for n, distances in enumerate(sequences):
            other = chip ^ jnp.where(core == 0, distances[0], distances[1])
            here = pl.ds(pl.multiple_of(other * 2 * inputs, LANES), 2 * inputs)
            lanes = slice(n * 2 * inputs, (n + 1) * 2 * inputs)
            result[slot, 0, :, here] = products[:inputs, lanes]
            result[slot, 1, :, here] = products[inputs:, lanes]

    pending = []
    held = None
    for start in range(0, slots, BATCH):
        batch = range(start, min(slots, start + BATCH))
        for slot in batch:
            correlate(slot)
        if held is None:
            owner_copy.wait()
            held = []
            for b in range(bands):
                hits = [(owner_ref[b, c] == band).astype(jnp.int32) for c in range(keep)]
                held.append(functools.reduce(lambda x, y: x + y, hits))
            total = functools.reduce(lambda x, y: x + y, held)
            for slot in range(RCAP):
                copy = pltpu.make_async_copy(zeros, out_ref.at[slot], zero_sems.at[slot])
                pl.when(slot >= total)(copy.start)
                pending.append((slot >= total, copy))
        for slot in batch:
            source = band ^ order[slot // slot_cap]
            rank = slot % slot_cap
            row = jnp.int32(rank)
            present = jnp.int32(0)
            for b in range(bands):
                row += jnp.where(b < source, held[b], 0)
                present += jnp.where(b == source, held[b], 0)
            copy = pltpu.make_async_copy(
                result.at[slot], out_ref.at[jnp.minimum(row, RCAP - 1)], sems.at[slot]
            )
            pl.when(rank < present)(copy.start)
            pending.append((rank < present, copy))
    for started, copy in pending:
        pl.when(started)(copy.wait)


def per_device(volts, taps, survive, owner):
    chan_count = lax.axis_size("chan")
    stn_count = lax.axis_size("stn")
    inputs, samples = volts.shape[2:]
    taps_count, fine_len = taps.shape
    keep = survive.shape[1]
    blocks = samples // fine_len
    times = blocks - taps_count + 1
    slot_cap = max(2, (RCAP + chan_count - 1) // chan_count)
    pack = max(1, LANES // inputs)
    lines = times // pack
    vmem = pl.BlockSpec(memory_space=pltpu.VMEM)
    anywhere = pl.BlockSpec(memory_space=pl.ANY)

    block = (slot_cap, 2 * lines, pack * inputs)
    pieces = pl.pallas_call(
        functools.partial(front_kernel, chan_count, slot_cap),
        out_shape=[jax.ShapeDtypeStruct(block, jnp.bfloat16)] * chan_count,
        in_specs=[anywhere] * 4,
        out_specs=[anywhere] * chan_count,
        scratch_shapes=[
            pltpu.VMEM((2, inputs, samples), jnp.bfloat16),
            pltpu.SMEM(survive.shape, jnp.int32),
            pltpu.SMEM(owner.shape, jnp.int32),
            pltpu.VMEM(taps.shape, jnp.float32),
            pltpu.VMEM((taps_count * 2 * keep, 2 * fine_len), jnp.bfloat16),
            pltpu.VMEM((taps_count * 2 * keep, -(-blocks // pack) * pack * inputs), jnp.float32),
            pltpu.VMEM((lines * 2 * keep, LANES), jnp.float32),
            pltpu.VMEM((chan_count,) + block, jnp.bfloat16),
            pltpu.SemaphoreType.DMA((len(group_sizes(blocks)),)),
            pltpu.SemaphoreType.DMA((3,)),
            pltpu.SemaphoreType.DMA((chan_count,)),
        ],
        compiler_params=pltpu.CompilerParams(vmem_limit_bytes=FRONT_VMEM),
    )(survive, owner, taps, volts)

    chips = list(range(stn_count // 2))
    order = [0] + list(range(2, chan_count)) + [1]
    out_shape = (RCAP, 2, inputs, stn_count * inputs)

    sequences = []
    for n in chips:
        other = n if n == 0 or (n == chips[-1] and n % 2) else n + 1 if n % 2 else n - 1
        sequences.append((n, other))

    def exchanged(block, distances):
        pairs = [(i, i ^ (2 * distances[i % 2])) for i in range(stn_count)]
        return lax.ppermute(block, "stn", pairs)

    def gathered(block):
        return [block] + [exchanged(block, pair) for pair in sequences[1:]]

    held = jnp.concatenate([pieces[0]] + [swapped(pieces[k], "chan", k) for k in order[1:]], 0)
    slots = held.shape[0]
    near = gathered(held)
    far = [swapped(x, "stn", 1) for x in near]
    visibilities = pl.pallas_call(
        functools.partial(back_kernel, sequences, order, slot_cap, times),
        out_shape=jax.ShapeDtypeStruct(out_shape, jnp.bfloat16),
        in_specs=[anywhere] + [vmem] * (2 * len(chips)),
        out_specs=anywhere,
        scratch_shapes=[
            pltpu.VMEM((slots,) + out_shape[1:], jnp.bfloat16),
            pltpu.VMEM(out_shape[1:], jnp.bfloat16),
            pltpu.SMEM(owner.shape, jnp.int32),
            pltpu.SemaphoreType.DMA(()),
            pltpu.SemaphoreType.DMA((slots,)),
            pltpu.SemaphoreType.DMA((RCAP,)),
        ],
        compiler_params=pltpu.CompilerParams(vmem_limit_bytes=BACK_VMEM),
    )(owner, *near, *far)
    return visibilities[None]


def solution(mesh):
    return jax.shard_map(
        per_device,
        mesh=mesh,
        in_specs=(P("chan", None, "stn", None), P(), P(), P()),
        out_specs=P("chan", None, None, "stn", None),
        check_vma=False,
    )
```

```python
import functools
import math

import jax
import jax.numpy as jnp
from jax import lax
from jax.experimental import pallas as pl
from jax.experimental.pallas import tpu as pltpu
from jax.sharding import PartitionSpec as P

RCAP = 24
LANES = 128
GROUPS = (24, 23)
FRONT_VMEM = 24 << 20
BACK_VMEM = 16 << 20


def swapped(x, axis, mask):
    peers = lax.axis_size(axis)
    return lax.ppermute(x, axis, [(i, i ^ mask) for i in range(peers)])


def group_sizes(blocks):
    groups, first = [], 0
    while first < blocks:
        count = min(GROUPS[min(len(groups), len(GROUPS) - 1)], blocks - first)
        groups.append((first, count))
        first += count
    return groups


def front_kernel(chan_count, survive_any, owner_any, taps_any, volts_ref, *rest):
    pieces, volts, survive_ref, owner_ref, taps_ref, table, products, spectra = rest[:-2]
    in_sems, small_sems = rest[-2:]
    taps_count, fine_len = taps_ref.shape
    inputs, samples = volts_ref.shape[2:]
    keep = survive_ref.shape[1]
    blocks = samples // fine_len
    times = blocks - taps_count + 1
    pack = max(1, LANES // inputs)
    lines = times // pack
    band = lax.axis_index("chan")
    core = lax.axis_index("stn") % 2

    small = []
    for n, (source, target) in enumerate(
        ((survive_any, survive_ref), (taps_any, taps_ref), (owner_any, owner_ref))
    ):
        copy = pltpu.make_async_copy(source, target, small_sems.at[n])
        copy.start()
        small.append(copy)
    groups = []
    for first, count in group_sizes(blocks):
        lanes = pl.ds(first * fine_len, count * fine_len)
        copy = pltpu.make_async_copy(
            volts_ref.at[0, :, :, lanes], volts.at[:, :, lanes], in_sems.at[len(groups)]
        )
        copy.start()
        groups.append((first, count, copy))

    small[0].wait()
    row_ids = lax.broadcasted_iota(jnp.int32, (keep, fine_len), 0)
    branch_ids = lax.broadcasted_iota(jnp.int32, (keep, fine_len), 1)
    chosen = jnp.zeros((keep, fine_len), jnp.int32)
    for c in range(keep):
        chosen = jnp.where(row_ids == c, survive_ref[band, c], chosen)
    angles = (chosen * branch_ids % fine_len).astype(jnp.float32) * (2.0 * math.pi / fine_len)
    factor = 1.0 / math.sqrt(fine_len)
    cosine = (jnp.cos(angles) * factor).astype(jnp.bfloat16).astype(jnp.float32)
    sine = (jnp.sin(angles) * factor).astype(jnp.bfloat16).astype(jnp.float32)
    real_row = jnp.concatenate([cosine, sine], 1)
    imag_row = jnp.concatenate([-sine, cosine], 1)
    both = jnp.concatenate([real_row, imag_row], 0)
    small[1].wait()
    for p in range(taps_count):
        tap = taps_ref[p : p + 1, :]
        table[p * 2 * keep : (p + 1) * 2 * keep, :] = (
            both * jnp.concatenate([tap, tap], 1)
        ).astype(jnp.bfloat16)

    pieces[...] = jnp.zeros_like(pieces)
    first_half = lax.broadcasted_iota(jnp.int32, (2 * keep, LANES), 1) < LANES // 2

    def finish(v):
        sums = [None] * (2 * pack - 1)
        for p in range(taps_count):
            for late in range(1 if p % pack == 0 else 2):
                u = v + p // pack + late
                which = 0 if p % pack == 0 else 1 + late
                term = products[p * 2 * keep : (p + 1) * 2 * keep, u * LANES : (u + 1) * LANES]
                sums[which] = term if sums[which] is None else sums[which] + term
        total = sums[0]
        if pack == 2:
            late = jnp.where(first_half, sums[2], sums[1])
            total = jnp.where(core == 0, total, late) + pltpu.roll(
                jnp.where(core == 0, late, total), LANES // 2, 1
            )
        spectra[v * 2 * keep : (v + 1) * 2 * keep, :] = total

    done = 0
    ready = 0
    for first, count, copy in groups:
        copy.wait()
        parts = []
        for s in range(first, first + count):
            lanes = slice(s * fine_len, (s + 1) * fine_len)
            parts.append(jnp.concatenate([volts[0, :, lanes], volts[1, :, lanes]], 1))
        if (count * inputs) % LANES:
            parts.append(parts[-1])
        end = first + len(parts)
        products[:, first * inputs : end * inputs] = lax.dot_general(
            table[...],
            jnp.concatenate(parts, 0),
            (((1,), (1,)), ((), ())),
            preferred_element_type=jnp.float32,
        )
        while done < ready:
            finish(done)
            done += 1
        ready = min(lines, max(0, end // pack - (taps_count - 1 + pack - 1) // pack))
    while done < lines:
        finish(done)
        done += 1

    small[2].wait()
    for c in range(keep):
        owner = owner_ref[band, c]
        rank = jnp.int32(0)
        for earlier in range(c):
            rank += (owner_ref[band, earlier] == owner).astype(jnp.int32)
        piece = owner ^ band
        for part in range(2):
            line = spectra[pl.ds(part * keep + c, lines, stride=2 * keep), :]
            pieces[piece, rank, part * lines : (part + 1) * lines, :] = line.astype(jnp.bfloat16)


def back_kernel(sequences, order, slot_cap, times, owner_ref, *rest):
    chips = len(sequences)
    near = rest[:chips]
    far = [rest[chips + sequences.index((m, n))] for n, m in sequences]
    out_ref, result, lefts, places, sems = rest[2 * chips :]
    bands, keep = owner_ref.shape
    slots = near[0].shape[0]
    inputs = out_ref.shape[2]
    band = lax.axis_index("chan")
    stn = lax.axis_index("stn")
    chip = stn // 2
    core = stn % 2
    pack = max(1, LANES // inputs)
    lines = times // pack

    bits = jnp.where(
        owner_ref[...] == band,
        jnp.left_shift(1, lax.broadcasted_iota(jnp.int32, (bands, keep), 1)).astype(jnp.float32),
        0.0,
    )
    held = [jnp.sum(bits[b : b + 1]).astype(jnp.int32) for b in range(bands)]

    lane = lax.broadcasted_iota(jnp.int32, (2 * lines, LANES), 1)
    low = lane < LANES // 2
    first = (lane // (LANES // 2)) == core

    def turn(x):
        return jnp.concatenate([x[:, LANES // 2 :], x[:, : LANES // 2]], 1)

    for place in range(slots):
        mine = near[0][place]
        turned = jnp.concatenate([mine[lines:], -mine[:lines]], 0)
        if pack == 1:
            lefts[place] = jnp.concatenate([mine, turned], 1)
        else:
            ahead = jnp.where(low, mine, turn(turned))
            behind = jnp.where(low, turn(mine), turned)
            lefts[place] = jnp.concatenate(
                [jnp.where(core == 0, ahead, behind), jnp.where(core == 0, behind, ahead)], 0
            )

    for slot in range(RCAP):
        places[slot] = 0
    total = jnp.int32(0)
    for b in range(bands):
        place = jnp.int32(0)
        for n, k in enumerate(order):
            place = jnp.where(b ^ band == k, n * slot_cap, place)
        for c in range(keep):
            mine = (held[b] >> c) & 1
            places[jnp.where(mine == 1, total, RCAP)] = place
            total += mine
            place += mine

    copies = []
    for slot in range(RCAP):
        place = places[slot]
        right = []
        for near_ref, far_ref in zip(near, far):
            x = near_ref[place]
            y = far_ref[place]
            if pack == 1:
                right.append(
                    jnp.concatenate([jnp.where(core == 0, x, y), jnp.where(core == 0, y, x)], 1)
                )
            else:
                right.append(
                    jnp.concatenate([jnp.where(first, x, y), turn(jnp.where(first, y, x))], 0)
                )
        products = lax.dot_general(
            lefts[place],
            jnp.concatenate(right, 1),
            (((0,), (0,)), ((), ())),
            preferred_element_type=jnp.float32,
        )
        products = jnp.where(slot < total, products * (1.0 / times), 0.0).astype(jnp.bfloat16)
        for n, distances in enumerate(sequences):
            other = chip ^ jnp.where(core == 0, distances[0], distances[1])
            here = pl.ds(pl.multiple_of(other * 2 * inputs, LANES), 2 * inputs)
            lanes = slice(n * 2 * inputs, (n + 1) * 2 * inputs)
            result[slot, 0, :, here] = products[:inputs, lanes]
            result[slot, 1, :, here] = products[inputs:, lanes]
        copy = pltpu.make_async_copy(result.at[slot], out_ref.at[slot], sems.at[slot])
        copy.start()
        copies.append(copy)
    for copy in copies:
        copy.wait()


def per_device(volts, taps, survive, owner):
    chan_count = lax.axis_size("chan")
    stn_count = lax.axis_size("stn")
    inputs, samples = volts.shape[2:]
    taps_count, fine_len = taps.shape
    keep = survive.shape[1]
    blocks = samples // fine_len
    times = blocks - taps_count + 1
    slot_cap = max(2, (RCAP + chan_count - 1) // chan_count)
    pack = max(1, LANES // inputs)
    lines = times // pack
    vmem = pl.BlockSpec(memory_space=pltpu.VMEM)
    anywhere = pl.BlockSpec(memory_space=pl.ANY)

    block = (slot_cap, 2 * lines, pack * inputs)
    pieces = pl.pallas_call(
        functools.partial(front_kernel, chan_count),
        out_shape=pltpu.VMEM((chan_count,) + block, jnp.bfloat16),
        in_specs=[pl.BlockSpec(memory_space=pltpu.HBM)] * 4,
        out_specs=vmem,
        scratch_shapes=[
            pltpu.VMEM((2, inputs, samples), jnp.bfloat16),
            pltpu.SMEM(survive.shape, jnp.int32),
            pltpu.SMEM(owner.shape, jnp.int32),
            pltpu.VMEM(taps.shape, jnp.float32),
            pltpu.VMEM((taps_count * 2 * keep, 2 * fine_len), jnp.bfloat16),
            pltpu.VMEM((taps_count * 2 * keep, -(-blocks // pack) * pack * inputs), jnp.float32),
            pltpu.VMEM((lines * 2 * keep, LANES), jnp.float32),
            pltpu.SemaphoreType.DMA((len(group_sizes(blocks)),)),
            pltpu.SemaphoreType.DMA((3,)),
        ],
        compiler_params=pltpu.CompilerParams(vmem_limit_bytes=FRONT_VMEM),
    )(*[pltpu.with_memory_space_constraint(x, pltpu.HBM) for x in (survive, owner, taps, volts)])

    chips = list(range(stn_count // 2))
    order = [0, 1] + list(range(chan_count - 1, 1, -1))
    out_shape = (RCAP, 2, inputs, stn_count * inputs)

    sequences = []
    for n in chips:
        other = n if n == 0 or (n == chips[-1] and n % 2) else n + 1 if n % 2 else n - 1
        sequences.append((n, other))

    def exchanged(block, distances):
        pairs = [(i, i ^ (2 * distances[i % 2])) for i in range(stn_count)]
        return lax.ppermute(block, "stn", pairs)

    def gathered(block):
        return [block] + [exchanged(block, pair) for pair in sequences[1:]]

    held = jnp.concatenate([pieces[0]] + [swapped(pieces[k], "chan", k) for k in order[1:]], 0)
    slots = held.shape[0]
    near = gathered(held)
    far = [swapped(x, "stn", 1) for x in near]
    visibilities = pl.pallas_call(
        functools.partial(back_kernel, sequences, order, slot_cap, times),
        out_shape=jax.ShapeDtypeStruct(out_shape, jnp.bfloat16),
        in_specs=[vmem] * (1 + 2 * len(chips)),
        out_specs=anywhere,
        scratch_shapes=[
            pltpu.VMEM(out_shape, jnp.bfloat16),
            pltpu.VMEM((slots, 2 * lines * pack, 2 * inputs), jnp.bfloat16),
            pltpu.SMEM((RCAP + 1,), jnp.int32),
            pltpu.SemaphoreType.DMA((RCAP,)),
        ],
        compiler_params=pltpu.CompilerParams(vmem_limit_bytes=BACK_VMEM),
    )(owner, *near, *far)
    return visibilities[None]


def solution(mesh):
    return jax.shard_map(
        per_device,
        mesh=mesh,
        in_specs=(P("chan", None, "stn", None), P(), P(), P()),
        out_specs=P("chan", None, None, "stn", None),
        check_vma=False,
    )
```

```python
import functools
import math

import jax
import jax.numpy as jnp
from jax import lax
from jax.experimental import pallas as pl
from jax.experimental.pallas import tpu as pltpu
from jax.sharding import PartitionSpec as P

RCAP = 24
LANES = 128
GROUPS = (16, 16, 15)
GROUP = 8
FRONT_VMEM = 24 << 20
BACK_VMEM = 16 << 20


def swapped(x, axis, mask):
    peers = lax.axis_size(axis)
    return lax.ppermute(x, axis, [(i, i ^ mask) for i in range(peers)])


def group_sizes(blocks):
    groups, first = [], 0
    while first < blocks:
        count = min(GROUPS[min(len(groups), len(GROUPS) - 1)], blocks - first)
        groups.append((first, count))
        first += count
    return groups


def front_kernel(chan_count, survive_any, owner_any, taps_any, volts_ref, *rest):
    pieces, volts, survive_ref, owner_ref, taps_ref, table, products, spectra = rest[:-2]
    in_sems, small_sems = rest[-2:]
    taps_count, fine_len = taps_ref.shape
    inputs, samples = volts_ref.shape[2:]
    keep = survive_ref.shape[1]
    blocks = samples // fine_len
    times = blocks - taps_count + 1
    pack = max(1, LANES // inputs)
    lines = times // pack
    band = lax.axis_index("chan")
    core = lax.axis_index("stn") % 2

    small = []
    for n, (source, target) in enumerate(
        ((survive_any, survive_ref), (taps_any, taps_ref), (owner_any, owner_ref))
    ):
        copy = pltpu.make_async_copy(source, target, small_sems.at[n])
        copy.start()
        small.append(copy)
    groups = []
    for first, count in group_sizes(blocks):
        lanes = pl.ds(first * fine_len, count * fine_len)
        copy = pltpu.make_async_copy(
            volts_ref.at[0, :, :, lanes], volts.at[:, :, lanes], in_sems.at[len(groups)]
        )
        copy.start()
        groups.append((first, count, copy))

    small[0].wait()
    row_ids = lax.broadcasted_iota(jnp.int32, (keep, fine_len), 0)
    branch_ids = lax.broadcasted_iota(jnp.int32, (keep, fine_len), 1)
    chosen = jnp.zeros((keep, fine_len), jnp.int32)
    for c in range(keep):
        chosen = jnp.where(row_ids == c, survive_ref[band, c], chosen)
    angles = (chosen * branch_ids % fine_len).astype(jnp.float32) * (2.0 * math.pi / fine_len)
    factor = 1.0 / math.sqrt(fine_len)
    cosine = (jnp.cos(angles) * factor).astype(jnp.bfloat16).astype(jnp.float32)
    sine = (jnp.sin(angles) * factor).astype(jnp.bfloat16).astype(jnp.float32)
    real_row = jnp.concatenate([cosine, sine], 1)
    imag_row = jnp.concatenate([-sine, cosine], 1)
    both = jnp.concatenate([real_row, imag_row], 0)
    small[1].wait()
    for p in range(taps_count):
        tap = taps_ref[p : p + 1, :]
        table[p * 2 * keep : (p + 1) * 2 * keep, :] = (
            both * jnp.concatenate([tap, tap], 1)
        ).astype(jnp.bfloat16)

    pieces[...] = jnp.zeros_like(pieces)
    first_half = lax.broadcasted_iota(jnp.int32, (2 * keep, LANES), 1) < LANES // 2

    def finish(v):
        sums = [None] * (2 * pack - 1)
        for p in range(taps_count):
            for late in range(1 if p % pack == 0 else 2):
                u = v + p // pack + late
                which = 0 if p % pack == 0 else 1 + late
                term = products[p * 2 * keep : (p + 1) * 2 * keep, u * LANES : (u + 1) * LANES]
                sums[which] = term if sums[which] is None else sums[which] + term
        total = sums[0]
        if pack == 2:
            late = jnp.where(first_half, sums[2], sums[1])
            total = jnp.where(core == 0, total, late) + pltpu.roll(
                jnp.where(core == 0, late, total), LANES // 2, 1
            )
        spectra[v * 2 * keep : (v + 1) * 2 * keep, :] = total

    done = 0
    ready = 0
    for first, count, copy in groups:
        copy.wait()
        end = first
        while end < first + count:
            parts = []
            for s in range(end, min(end + GROUP, first + count)):
                lanes = slice(s * fine_len, (s + 1) * fine_len)
                parts.append(jnp.concatenate([volts[0, :, lanes], volts[1, :, lanes]], 1))
            if (len(parts) * inputs) % LANES:
                parts.append(parts[-1])
            products[:, end * inputs : (end + len(parts)) * inputs] = lax.dot_general(
                table[...],
                jnp.concatenate(parts, 0),
                (((1,), (1,)), ((), ())),
                preferred_element_type=jnp.float32,
            )
            end += len(parts)
        while done < ready:
            finish(done)
            done += 1
        ready = min(lines, max(0, end // pack - (taps_count - 1 + pack - 1) // pack))
    while done < lines:
        finish(done)
        done += 1

    small[2].wait()
    for c in range(keep):
        owner = owner_ref[band, c]
        rank = jnp.int32(0)
        for earlier in range(c):
            rank += (owner_ref[band, earlier] == owner).astype(jnp.int32)
        piece = owner ^ band
        for part in range(2):
            line = spectra[pl.ds(part * keep + c, lines, stride=2 * keep), :]
            pieces[piece, rank, part * lines : (part + 1) * lines, :] = line.astype(jnp.bfloat16)


def turn(x):
    return jnp.concatenate([x[:, LANES // 2 :], x[:, : LANES // 2]], 1)


def left_kernel(inputs, order, slot_cap, owner_ref, held_ref, lefts, places):
    bands, keep = owner_ref.shape
    band = lax.axis_index("chan")
    core = lax.axis_index("stn") % 2
    slots, lines = held_ref.shape[0], held_ref.shape[1] // 2
    low = lax.broadcasted_iota(jnp.int32, (2 * lines, LANES), 1) < LANES // 2
    for place in range(slots):
        mine = held_ref[place]
        turned = jnp.concatenate([mine[lines:], -mine[:lines]], 0)
        if inputs >= LANES:
            lefts[place] = jnp.concatenate([mine, turned], 1)
        else:
            ahead = jnp.where(low, mine, turn(turned))
            behind = jnp.where(low, turn(mine), turned)
            lefts[place] = jnp.concatenate(
                [jnp.where(core == 0, ahead, behind), jnp.where(core == 0, behind, ahead)], 0
            )

    bits = jnp.where(
        owner_ref[...] == band,
        jnp.left_shift(1, lax.broadcasted_iota(jnp.int32, (bands, keep), 1)).astype(jnp.float32),
        0.0,
    )
    held = [jnp.sum(bits[b : b + 1]).astype(jnp.int32) for b in range(bands)]

    for slot in range(RCAP):
        places[slot] = 0
    total = jnp.int32(0)
    for b in range(bands):
        place = jnp.int32(0)
        for n, k in enumerate(order):
            place = jnp.where(b ^ band == k, n * slot_cap, place)
        for c in range(keep):
            mine = (held[b] >> c) & 1
            places[jnp.where(mine == 1, total, RCAP)] = place
            total += mine
            place += mine
    places[RCAP + 1] = total


def back_kernel(sequences, times, places, *rest):
    chips = len(sequences)
    near = rest[:chips]
    far = [rest[chips + sequences.index((m, n))] for n, m in sequences]
    lefts, out_ref, result, sems = rest[2 * chips :]
    inputs = out_ref.shape[2]
    stn = lax.axis_index("stn")
    chip = stn // 2
    core = stn % 2
    pack = max(1, LANES // inputs)
    lines = times // pack

    lane = lax.broadcasted_iota(jnp.int32, (2 * lines, LANES), 1)
    first = (lane // (LANES // 2)) == core

    total = places[RCAP + 1]
    copies = []
    for slot in range(RCAP):
        place = places[slot]
        right = []
        for near_ref, far_ref in zip(near, far):
            x = near_ref[place]
            y = far_ref[place]
            if pack == 1:
                right.append(
                    jnp.concatenate([jnp.where(core == 0, x, y), jnp.where(core == 0, y, x)], 1)
                )
            else:
                right.append(
                    jnp.concatenate([jnp.where(first, x, y), turn(jnp.where(first, y, x))], 0)
                )
        products = lax.dot_general(
            lefts[place],
            jnp.concatenate(right, 1),
            (((0,), (0,)), ((), ())),
            preferred_element_type=jnp.float32,
        )
        products = jnp.where(slot < total, products * (1.0 / times), 0.0).astype(jnp.bfloat16)
        for n, distances in enumerate(sequences):
            other = chip ^ jnp.where(core == 0, distances[0], distances[1])
            here = pl.ds(pl.multiple_of(other * 2 * inputs, LANES), 2 * inputs)
            lanes = slice(n * 2 * inputs, (n + 1) * 2 * inputs)
            result[slot, 0, :, here] = products[:inputs, lanes]
            result[slot, 1, :, here] = products[inputs:, lanes]
        copy = pltpu.make_async_copy(result.at[slot], out_ref.at[slot], sems.at[slot])
        copy.start()
        copies.append(copy)
    for copy in copies:
        copy.wait()


def per_device(volts, taps, survive, owner):
    chan_count = lax.axis_size("chan")
    stn_count = lax.axis_size("stn")
    inputs, samples = volts.shape[2:]
    taps_count, fine_len = taps.shape
    keep = survive.shape[1]
    blocks = samples // fine_len
    times = blocks - taps_count + 1
    slot_cap = max(2, (RCAP + chan_count - 1) // chan_count)
    pack = max(1, LANES // inputs)
    lines = times // pack
    vmem = pl.BlockSpec(memory_space=pltpu.VMEM)
    smem = pl.BlockSpec(memory_space=pltpu.SMEM)
    anywhere = pl.BlockSpec(memory_space=pl.ANY)

    block = (slot_cap, 2 * lines, pack * inputs)
    pieces = pl.pallas_call(
        functools.partial(front_kernel, chan_count),
        out_shape=pltpu.VMEM((chan_count,) + block, jnp.bfloat16),
        in_specs=[pl.BlockSpec(memory_space=pltpu.HBM)] * 4,
        out_specs=vmem,
        scratch_shapes=[
            pltpu.VMEM((2, inputs, samples), jnp.bfloat16),
            pltpu.SMEM(survive.shape, jnp.int32),
            pltpu.SMEM(owner.shape, jnp.int32),
            pltpu.VMEM(taps.shape, jnp.float32),
            pltpu.VMEM((taps_count * 2 * keep, 2 * fine_len), jnp.bfloat16),
            pltpu.VMEM((taps_count * 2 * keep, -(-blocks // pack) * pack * inputs), jnp.float32),
            pltpu.VMEM((lines * 2 * keep, LANES), jnp.float32),
            pltpu.SemaphoreType.DMA((len(group_sizes(blocks)),)),
            pltpu.SemaphoreType.DMA((3,)),
        ],
        compiler_params=pltpu.CompilerParams(vmem_limit_bytes=FRONT_VMEM),
    )(*[pltpu.with_memory_space_constraint(x, pltpu.HBM) for x in (survive, owner, taps, volts)])

    chips = list(range(stn_count // 2))
    order = [0, 1] + list(range(chan_count - 1, 1, -1))
    out_shape = (RCAP, 2, inputs, stn_count * inputs)

    sequences = []
    for n in chips:
        other = n if n == 0 or (n == chips[-1] and n % 2) else n + 1 if n % 2 else n - 1
        sequences.append((n, other))

    def exchanged(block, distances):
        pairs = [(i, i ^ (2 * distances[i % 2])) for i in range(stn_count)]
        return lax.ppermute(block, "stn", pairs)

    def gathered(block):
        return [block] + [exchanged(block, pair) for pair in sequences[1:]]

    held = jnp.concatenate([pieces[0]] + [swapped(pieces[k], "chan", k) for k in order[1:]], 0)
    slots = held.shape[0]
    near = gathered(held)
    far = [swapped(x, "stn", 1) for x in near]
    lefts, places = pl.pallas_call(
        functools.partial(left_kernel, inputs, order, slot_cap),
        out_shape=[
            pltpu.VMEM((slots, 2 * lines * pack, 2 * inputs), jnp.bfloat16),
            pltpu.SMEM((RCAP + 2,), jnp.int32),
        ],
        in_specs=[vmem] * 2,
        out_specs=[vmem, smem],
        compiler_params=pltpu.CompilerParams(vmem_limit_bytes=BACK_VMEM),
    )(owner, held)
    visibilities = pl.pallas_call(
        functools.partial(back_kernel, sequences, times),
        out_shape=jax.ShapeDtypeStruct(out_shape, jnp.bfloat16),
        in_specs=[smem] + [vmem] * (1 + 2 * len(chips)),
        out_specs=anywhere,
        scratch_shapes=[
            pltpu.VMEM(out_shape, jnp.bfloat16),
            pltpu.SemaphoreType.DMA((RCAP,)),
        ],
        compiler_params=pltpu.CompilerParams(vmem_limit_bytes=BACK_VMEM),
    )(places, *near, *far, lefts)
    return visibilities[None]


def solution(mesh):
    return jax.shard_map(
        per_device,
        mesh=mesh,
        in_specs=(P("chan", None, "stn", None), P(), P(), P()),
        out_specs=P("chan", None, None, "stn", None),
        check_vma=False,
    )
```

```python
import functools
import math

import jax
import jax.numpy as jnp
from jax import lax
from jax.experimental import pallas as pl
from jax.experimental.pallas import tpu as pltpu
from jax.sharding import PartitionSpec as P

RCAP = 24
LANES = 128
GROUPS = (16, 16, 15)
GROUP = 8
FRONT_VMEM = 24 << 20
BACK_VMEM = 16 << 20


def swapped(x, axis, mask):
    peers = lax.axis_size(axis)
    return lax.ppermute(x, axis, [(i, i ^ mask) for i in range(peers)])


def group_sizes(blocks):
    groups, first = [], 0
    while first < blocks:
        count = min(GROUPS[min(len(groups), len(GROUPS) - 1)], blocks - first)
        groups.append((first, count))
        first += count
    return groups


def front_kernel(chan_count, survive_any, owner_any, taps_any, volts_ref, *rest):
    pieces, volts, survive_ref, owner_ref, taps_ref, table, products, spectra = rest[:-2]
    in_sems, small_sems = rest[-2:]
    taps_count, fine_len = taps_ref.shape
    inputs, samples = volts_ref.shape[2:]
    keep = survive_ref.shape[1]
    blocks = samples // fine_len
    times = blocks - taps_count + 1
    pack = max(1, LANES // inputs)
    lines = times // pack
    band = lax.axis_index("chan")
    core = lax.axis_index("stn") % 2

    small = []
    for n, (source, target) in enumerate(
        ((survive_any, survive_ref), (taps_any, taps_ref), (owner_any, owner_ref))
    ):
        copy = pltpu.make_async_copy(source, target, small_sems.at[n])
        copy.start()
        small.append(copy)
    groups = []
    for first, count in group_sizes(blocks):
        lanes = pl.ds(first * fine_len, count * fine_len)
        copy = pltpu.make_async_copy(
            volts_ref.at[0, :, :, lanes], volts.at[:, :, lanes], in_sems.at[len(groups)]
        )
        copy.start()
        groups.append((first, count, copy))

    small[0].wait()
    row_ids = lax.broadcasted_iota(jnp.int32, (keep, fine_len), 0)
    branch_ids = lax.broadcasted_iota(jnp.int32, (keep, fine_len), 1)
    chosen = jnp.zeros((keep, fine_len), jnp.int32)
    for c in range(keep):
        chosen = jnp.where(row_ids == c, survive_ref[band, c], chosen)
    angles = (chosen * branch_ids % fine_len).astype(jnp.float32) * (2.0 * math.pi / fine_len)
    factor = 1.0 / math.sqrt(fine_len)
    cosine = (jnp.cos(angles) * factor).astype(jnp.bfloat16).astype(jnp.float32)
    sine = (jnp.sin(angles) * factor).astype(jnp.bfloat16).astype(jnp.float32)
    real_row = jnp.concatenate([cosine, sine], 1)
    imag_row = jnp.concatenate([-sine, cosine], 1)
    both = jnp.concatenate([real_row, imag_row], 0)
    small[1].wait()
    for p in range(taps_count):
        tap = taps_ref[p : p + 1, :]
        table[p * 2 * keep : (p + 1) * 2 * keep, :] = (
            both * jnp.concatenate([tap, tap], 1)
        ).astype(jnp.bfloat16)

    pieces[...] = jnp.zeros_like(pieces)
    first_half = lax.broadcasted_iota(jnp.int32, (2 * keep, LANES), 1) < LANES // 2

    def finish(v):
        sums = [None] * (2 * pack - 1)
        for p in range(taps_count):
            for late in range(1 if p % pack == 0 else 2):
                u = v + p // pack + late
                which = 0 if p % pack == 0 else 1 + late
                term = products[p * 2 * keep : (p + 1) * 2 * keep, u * LANES : (u + 1) * LANES]
                sums[which] = term if sums[which] is None else sums[which] + term
        total = sums[0]
        if pack == 2:
            late = jnp.where(first_half, sums[2], sums[1])
            total = jnp.where(core == 0, total, late) + pltpu.roll(
                jnp.where(core == 0, late, total), LANES // 2, 1
            )
        spectra[v * 2 * keep : (v + 1) * 2 * keep, :] = total

    done = 0
    ready = 0
    for first, count, copy in groups:
        copy.wait()
        end = first
        while end < first + count:
            parts = []
            for s in range(end, min(end + GROUP, first + count)):
                lanes = slice(s * fine_len, (s + 1) * fine_len)
                parts.append(jnp.concatenate([volts[0, :, lanes], volts[1, :, lanes]], 1))
            if (len(parts) * inputs) % LANES:
                parts.append(parts[-1])
            products[:, end * inputs : (end + len(parts)) * inputs] = lax.dot_general(
                table[...],
                jnp.concatenate(parts, 0),
                (((1,), (1,)), ((), ())),
                preferred_element_type=jnp.float32,
            )
            end += len(parts)
        while done < ready:
            finish(done)
            done += 1
        ready = min(lines, max(0, end // pack - (taps_count - 1 + pack - 1) // pack))
    while done < lines:
        finish(done)
        done += 1

    small[2].wait()
    for c in range(keep):
        owner = owner_ref[band, c]
        rank = jnp.int32(0)
        for earlier in range(c):
            rank += (owner_ref[band, earlier] == owner).astype(jnp.int32)
        piece = owner ^ band
        for part in range(2):
            line = spectra[pl.ds(part * keep + c, lines, stride=2 * keep), :]
            pieces[piece, rank, part * lines : (part + 1) * lines, :] = line.astype(jnp.bfloat16)


def turn(x):
    return jnp.concatenate([x[:, LANES // 2 :], x[:, : LANES // 2]], 1)


def fill(result, slot, place, total, times, members, near, far, lefts):
    stn = lax.axis_index("stn")
    chip = stn // 2
    core = stn % 2
    inputs = result.shape[2]
    lane = lax.broadcasted_iota(jnp.int32, near[0].shape[1:], 1)
    first = (lane // (LANES // 2)) == core
    right = []
    for near_ref, far_ref in zip(near, far):
        x = near_ref[place]
        y = far_ref[place]
        if inputs >= LANES:
            right.append(
                jnp.concatenate([jnp.where(core == 0, x, y), jnp.where(core == 0, y, x)], 1)
            )
        else:
            right.append(jnp.concatenate([jnp.where(first, x, y), turn(jnp.where(first, y, x))], 0))
    products = lax.dot_general(
        lefts[place],
        jnp.concatenate(right, 1),
        (((1,), (0,)), ((), ())),
        preferred_element_type=jnp.float32,
    )
    products = jnp.where(slot < total, products * (1.0 / times), 0.0).astype(jnp.bfloat16)
    for n, distances in enumerate(members):
        other = chip ^ jnp.where(core == 0, distances[0], distances[1])
        here = pl.ds(pl.multiple_of(other * 2 * inputs, LANES), 2 * inputs)
        lanes = slice(n * 2 * inputs, (n + 1) * 2 * inputs)
        result[slot, 0, :, here] = products[:inputs, lanes]
        result[slot, 1, :, here] = products[inputs:, lanes]


def first_kernel(members, order, slot_cap, times, owner_ref, *rest):
    near = rest[: len(members)]
    far = rest[len(members) : 2 * len(members)]
    lefts, places, result = rest[2 * len(members) :]
    held_ref = near[0]
    inputs = result.shape[2]
    bands, keep = owner_ref.shape
    band = lax.axis_index("chan")
    core = lax.axis_index("stn") % 2
    slots, lines = held_ref.shape[0], held_ref.shape[1] // 2
    low = lax.broadcasted_iota(jnp.int32, (2 * lines, LANES), 1) < LANES // 2
    for place in range(slots):
        mine = held_ref[place]
        turned = jnp.concatenate([mine[lines:], -mine[:lines]], 0)
        if inputs >= LANES:
            left = jnp.concatenate([mine, turned], 1)
        else:
            ahead = jnp.where(low, mine, turn(turned))
            behind = jnp.where(low, turn(mine), turned)
            left = jnp.concatenate(
                [jnp.where(core == 0, ahead, behind), jnp.where(core == 0, behind, ahead)], 0
            )
        lefts[place] = left.T

    bits = jnp.where(
        owner_ref[...] == band,
        jnp.left_shift(1, lax.broadcasted_iota(jnp.int32, (bands, keep), 1)).astype(jnp.float32),
        0.0,
    )
    held = [jnp.sum(bits[b : b + 1]).astype(jnp.int32) for b in range(bands)]

    for slot in range(RCAP):
        places[slot] = 0
    total = jnp.int32(0)
    for b in range(bands):
        place = jnp.int32(0)
        for n, k in enumerate(order):
            place = jnp.where(b ^ band == k, n * slot_cap, place)
        for c in range(keep):
            mine = (held[b] >> c) & 1
            places[jnp.where(mine == 1, total, RCAP)] = place
            total += mine
            place += mine
    places[RCAP + 1] = total
    for slot in range(RCAP):
        fill(result, slot, places[slot], total, times, members, near, far, lefts)


def back_kernel(members, times, places, *rest):
    near = rest[: len(members)]
    far = [rest[len(members) + members.index((m, n))] for n, m in members]
    lefts = rest[2 * len(members)]
    out_ref, result, sems = rest[-3:]
    total = places[RCAP + 1]
    copies = []
    for slot in range(RCAP):
        fill(result, slot, places[slot], total, times, members, near, far, lefts)
        copy = pltpu.make_async_copy(result.at[slot], out_ref.at[slot], sems.at[slot])
        copy.start()
        copies.append(copy)
    for copy in copies:
        copy.wait()


def per_device(volts, taps, survive, owner):
    chan_count = lax.axis_size("chan")
    stn_count = lax.axis_size("stn")
    inputs, samples = volts.shape[2:]
    taps_count, fine_len = taps.shape
    keep = survive.shape[1]
    blocks = samples // fine_len
    times = blocks - taps_count + 1
    slot_cap = max(2, (RCAP + chan_count - 1) // chan_count)
    pack = max(1, LANES // inputs)
    lines = times // pack
    vmem = pl.BlockSpec(memory_space=pltpu.VMEM)
    smem = pl.BlockSpec(memory_space=pltpu.SMEM)
    anywhere = pl.BlockSpec(memory_space=pl.ANY)

    block = (slot_cap, 2 * lines, pack * inputs)
    pieces = pl.pallas_call(
        functools.partial(front_kernel, chan_count),
        out_shape=pltpu.VMEM((chan_count,) + block, jnp.bfloat16),
        in_specs=[pl.BlockSpec(memory_space=pltpu.HBM)] * 4,
        out_specs=vmem,
        scratch_shapes=[
            pltpu.VMEM((2, inputs, samples), jnp.bfloat16),
            pltpu.SMEM(survive.shape, jnp.int32),
            pltpu.SMEM(owner.shape, jnp.int32),
            pltpu.VMEM(taps.shape, jnp.float32),
            pltpu.VMEM((taps_count * 2 * keep, 2 * fine_len), jnp.bfloat16),
            pltpu.VMEM((taps_count * 2 * keep, -(-blocks // pack) * pack * inputs), jnp.float32),
            pltpu.VMEM((lines * 2 * keep, LANES), jnp.float32),
            pltpu.SemaphoreType.DMA((len(group_sizes(blocks)),)),
            pltpu.SemaphoreType.DMA((3,)),
        ],
        compiler_params=pltpu.CompilerParams(vmem_limit_bytes=FRONT_VMEM),
    )(*[pltpu.with_memory_space_constraint(x, pltpu.HBM) for x in (survive, owner, taps, volts)])

    chips = list(range(stn_count // 2))
    order = [0, 1] + list(range(chan_count - 1, 1, -1))
    out_shape = (RCAP, 2, inputs, stn_count * inputs)

    sequences = []
    for n in chips:
        other = n if n == 0 or (n == chips[-1] and n % 2) else n + 1 if n % 2 else n - 1
        sequences.append((n, other))

    def exchanged(block, distances):
        pairs = [(i, i ^ (2 * distances[i % 2])) for i in range(stn_count)]
        return lax.ppermute(block, "stn", pairs)

    def gathered(block):
        return [block] + [exchanged(block, pair) for pair in sequences[1:]]

    held = jnp.concatenate([pieces[0]] + [swapped(pieces[k], "chan", k) for k in order[1:]], 0)
    slots = held.shape[0]
    near = gathered(held)
    far = [swapped(x, "stn", 1) for x in near]
    ahead, behind = [0, chips[-1]], chips[1:-1]
    lefts, places, result = pl.pallas_call(
        functools.partial(first_kernel, [sequences[n] for n in ahead], order, slot_cap, times),
        out_shape=[
            pltpu.VMEM((slots, 2 * inputs, 2 * lines * pack), jnp.bfloat16),
            pltpu.SMEM((RCAP + 2,), jnp.int32),
            pltpu.VMEM(out_shape, jnp.bfloat16),
        ],
        in_specs=[vmem] * (1 + 2 * len(ahead)),
        out_specs=[vmem, smem, vmem],
        compiler_params=pltpu.CompilerParams(vmem_limit_bytes=BACK_VMEM),
    )(owner, *[near[n] for n in ahead], *[far[n] for n in ahead])
    visibilities, _ = pl.pallas_call(
        functools.partial(back_kernel, [sequences[n] for n in behind], times),
        out_shape=[jax.ShapeDtypeStruct(out_shape, jnp.bfloat16), pltpu.VMEM(out_shape, jnp.bfloat16)],
        in_specs=[smem] + [vmem] * (2 + 2 * len(behind)),
        out_specs=[anywhere, vmem],
        input_output_aliases={2 + 2 * len(behind): 1},
        scratch_shapes=[pltpu.SemaphoreType.DMA((RCAP,))],
        compiler_params=pltpu.CompilerParams(vmem_limit_bytes=BACK_VMEM),
    )(places, *[near[n] for n in behind], *[far[n] for n in behind], lefts, result)
    return visibilities[None]


def solution(mesh):
    return jax.shard_map(
        per_device,
        mesh=mesh,
        in_specs=(P("chan", None, "stn", None), P(), P(), P()),
        out_specs=P("chan", None, None, "stn", None),
        check_vma=False,
    )
```

```python
import functools
import math

import jax
import jax.numpy as jnp
from jax import lax
from jax.experimental import pallas as pl
from jax.experimental.pallas import tpu as pltpu
from jax.sharding import PartitionSpec as P

RCAP = 24
LANES = 128
GROUPS = (16, 16, 15)
GROUP = 8
FRONT_VMEM = 24 << 20
BACK_VMEM = 16 << 20


def swapped(x, axis, mask):
    peers = lax.axis_size(axis)
    return lax.ppermute(x, axis, [(i, i ^ mask) for i in range(peers)])


def group_sizes(blocks):
    groups, first = [], 0
    while first < blocks:
        count = min(GROUPS[min(len(groups), len(GROUPS) - 1)], blocks - first)
        groups.append((first, count))
        first += count
    return groups


def front_kernel(chan_count, survive_any, owner_any, taps_any, volts_ref, *rest):
    pieces, volts, survive_ref, owner_ref, taps_ref, table, products, spectra = rest[:-2]
    in_sems, small_sems = rest[-2:]
    taps_count, fine_len = taps_ref.shape
    inputs, samples = volts_ref.shape[2:]
    keep = survive_ref.shape[1]
    blocks = samples // fine_len
    times = blocks - taps_count + 1
    pack = max(1, LANES // inputs)
    lines = times // pack
    band = lax.axis_index("chan")
    core = lax.axis_index("stn") % 2

    small = []
    for n, (source, target) in enumerate(
        ((survive_any, survive_ref), (taps_any, taps_ref), (owner_any, owner_ref))
    ):
        copy = pltpu.make_async_copy(source, target, small_sems.at[n])
        copy.start()
        small.append(copy)
    groups = []
    for first, count in group_sizes(blocks):
        lanes = pl.ds(first * fine_len, count * fine_len)
        copy = pltpu.make_async_copy(
            volts_ref.at[0, :, :, lanes], volts.at[:, :, lanes], in_sems.at[len(groups)]
        )
        copy.start()
        groups.append((first, count, copy))

    small[0].wait()
    row_ids = lax.broadcasted_iota(jnp.int32, (keep, fine_len), 0)
    branch_ids = lax.broadcasted_iota(jnp.int32, (keep, fine_len), 1)
    chosen = jnp.zeros((keep, fine_len), jnp.int32)
    for c in range(keep):
        chosen = jnp.where(row_ids == c, survive_ref[band, c], chosen)
    angles = (chosen * branch_ids % fine_len).astype(jnp.float32) * (2.0 * math.pi / fine_len)
    factor = 1.0 / math.sqrt(fine_len)
    cosine = (jnp.cos(angles) * factor).astype(jnp.bfloat16).astype(jnp.float32)
    sine = (jnp.sin(angles) * factor).astype(jnp.bfloat16).astype(jnp.float32)
    real_row = jnp.concatenate([cosine, sine], 1)
    imag_row = jnp.concatenate([-sine, cosine], 1)
    both = jnp.concatenate([real_row, imag_row], 0)
    small[1].wait()
    for p in range(taps_count):
        tap = taps_ref[p : p + 1, :]
        table[p * 2 * keep : (p + 1) * 2 * keep, :] = (
            both * jnp.concatenate([tap, tap], 1)
        ).astype(jnp.bfloat16)

    pieces[...] = jnp.zeros_like(pieces)
    first_half = lax.broadcasted_iota(jnp.int32, (2 * keep, LANES), 1) < LANES // 2

    def finish(v):
        sums = [None] * (2 * pack - 1)
        for p in range(taps_count):
            for late in range(1 if p % pack == 0 else 2):
                u = v + p // pack + late
                which = 0 if p % pack == 0 else 1 + late
                term = products[p * 2 * keep : (p + 1) * 2 * keep, u * LANES : (u + 1) * LANES]
                sums[which] = term if sums[which] is None else sums[which] + term
        total = sums[0]
        if pack == 2:
            late = jnp.where(first_half, sums[2], sums[1])
            total = jnp.where(core == 0, total, late) + pltpu.roll(
                jnp.where(core == 0, late, total), LANES // 2, 1
            )
        spectra[v * 2 * keep : (v + 1) * 2 * keep, :] = total

    done = 0
    ready = 0
    for first, count, copy in groups:
        copy.wait()
        end = first
        while end < first + count:
            parts = []
            for s in range(end, min(end + GROUP, first + count)):
                lanes = slice(s * fine_len, (s + 1) * fine_len)
                parts.append(jnp.concatenate([volts[0, :, lanes], volts[1, :, lanes]], 1))
            if (len(parts) * inputs) % LANES:
                parts.append(parts[-1])
            products[:, end * inputs : (end + len(parts)) * inputs] = lax.dot_general(
                table[...],
                jnp.concatenate(parts, 0),
                (((1,), (1,)), ((), ())),
                preferred_element_type=jnp.float32,
            )
            end += len(parts)
        while done < ready:
            finish(done)
            done += 1
        ready = min(lines, max(0, end // pack - (taps_count - 1 + pack - 1) // pack))
    while done < lines:
        finish(done)
        done += 1

    small[2].wait()
    for c in range(keep):
        owner = owner_ref[band, c]
        rank = jnp.int32(0)
        for earlier in range(c):
            rank += (owner_ref[band, earlier] == owner).astype(jnp.int32)
        piece = owner ^ band
        both = [spectra[pl.ds(part * keep + c, lines, stride=2 * keep), :] for part in range(2)]
        pieces[piece, rank] = jnp.concatenate(both, 0).astype(jnp.bfloat16)


def turn(x):
    return jnp.concatenate([x[:, LANES // 2 :], x[:, : LANES // 2]], 1)


def fill(result, slot, place, total, times, members, near, far, lefts):
    stn = lax.axis_index("stn")
    chip = stn // 2
    core = stn % 2
    inputs = result.shape[2]
    lane = lax.broadcasted_iota(jnp.int32, near[0].shape[1:], 1)
    first = (lane // (LANES // 2)) == core
    right = []
    for near_ref, far_ref in zip(near, far):
        x = near_ref[place]
        y = far_ref[place]
        if inputs >= LANES:
            right.append(
                jnp.concatenate([jnp.where(core == 0, x, y), jnp.where(core == 0, y, x)], 1)
            )
        else:
            right.append(jnp.concatenate([jnp.where(first, x, y), turn(jnp.where(first, y, x))], 0))
    products = lax.dot_general(
        lefts[place],
        jnp.concatenate(right, 1),
        (((1,), (0,)), ((), ())),
        preferred_element_type=jnp.float32,
    )
    products = jnp.where(slot < total, products * (1.0 / times), 0.0).astype(jnp.bfloat16)
    for n, distances in enumerate(members):
        other = chip ^ jnp.where(core == 0, distances[0], distances[1])
        here = pl.ds(pl.multiple_of(other * 2 * inputs, LANES), 2 * inputs)
        lanes = slice(n * 2 * inputs, (n + 1) * 2 * inputs)
        result[slot, 0, :, here] = products[:inputs, lanes]
        result[slot, 1, :, here] = products[inputs:, lanes]


def first_kernel(members, order, slot_cap, times, owner_ref, *rest):
    near = rest[: len(members)]
    far = rest[len(members) : 2 * len(members)]
    lefts, places, result = rest[2 * len(members) :]
    held_ref = near[0]
    inputs = result.shape[2]
    bands, keep = owner_ref.shape
    band = lax.axis_index("chan")
    core = lax.axis_index("stn") % 2
    slots, lines = held_ref.shape[0], held_ref.shape[1] // 2
    low = lax.broadcasted_iota(jnp.int32, (2 * lines, LANES), 1) < LANES // 2
    for place in range(slots):
        mine = held_ref[place]
        turned = jnp.concatenate([mine[lines:], -mine[:lines]], 0)
        if inputs >= LANES:
            left = jnp.concatenate([mine, turned], 1)
        else:
            ahead = jnp.where(low, mine, turn(turned))
            behind = jnp.where(low, turn(mine), turned)
            left = jnp.concatenate(
                [jnp.where(core == 0, ahead, behind), jnp.where(core == 0, behind, ahead)], 0
            )
        lefts[place] = left.T

    bits = jnp.where(
        owner_ref[...] == band,
        jnp.left_shift(1, lax.broadcasted_iota(jnp.int32, (bands, keep), 1)).astype(jnp.float32),
        0.0,
    )
    held = [jnp.sum(bits[b : b + 1]).astype(jnp.int32) for b in range(bands)]

    for slot in range(RCAP):
        places[slot] = 0
    total = jnp.int32(0)
    for b in range(bands):
        place = jnp.int32(0)
        for n, k in enumerate(order):
            place = jnp.where(b ^ band == k, n * slot_cap, place)
        for c in range(keep):
            mine = (held[b] >> c) & 1
            places[jnp.where(mine == 1, total, RCAP)] = place
            total += mine
            place += mine
    places[RCAP + 1] = total
    for slot in range(RCAP):
        fill(result, slot, places[slot], total, times, members, near, far, lefts)


def back_kernel(members, times, places, *rest):
    near = rest[: len(members)]
    far = [rest[len(members) + members.index((m, n))] for n, m in members]
    lefts = rest[2 * len(members)]
    out_ref, result, sems = rest[-3:]
    total = places[RCAP + 1]
    copies = []
    for slot in range(RCAP):
        fill(result, slot, places[slot], total, times, members, near, far, lefts)
        copy = pltpu.make_async_copy(result.at[slot], out_ref.at[slot], sems.at[slot])
        copy.start()
        copies.append(copy)
    for copy in copies:
        copy.wait()


def per_device(volts, taps, survive, owner):
    chan_count = lax.axis_size("chan")
    stn_count = lax.axis_size("stn")
    inputs, samples = volts.shape[2:]
    taps_count, fine_len = taps.shape
    keep = survive.shape[1]
    blocks = samples // fine_len
    times = blocks - taps_count + 1
    slot_cap = max(2, (RCAP + chan_count - 1) // chan_count)
    pack = max(1, LANES // inputs)
    lines = times // pack
    vmem = pl.BlockSpec(memory_space=pltpu.VMEM)
    smem = pl.BlockSpec(memory_space=pltpu.SMEM)
    anywhere = pl.BlockSpec(memory_space=pl.ANY)

    block = (slot_cap, 2 * lines, pack * inputs)
    pieces = pl.pallas_call(
        functools.partial(front_kernel, chan_count),
        out_shape=pltpu.VMEM((chan_count,) + block, jnp.bfloat16),
        in_specs=[pl.BlockSpec(memory_space=pltpu.HBM)] * 4,
        out_specs=vmem,
        scratch_shapes=[
            pltpu.VMEM((2, inputs, samples), jnp.bfloat16),
            pltpu.SMEM(survive.shape, jnp.int32),
            pltpu.SMEM(owner.shape, jnp.int32),
            pltpu.VMEM(taps.shape, jnp.float32),
            pltpu.VMEM((taps_count * 2 * keep, 2 * fine_len), jnp.bfloat16),
            pltpu.VMEM((taps_count * 2 * keep, -(-blocks // pack) * pack * inputs), jnp.float32),
            pltpu.VMEM((lines * 2 * keep, LANES), jnp.float32),
            pltpu.SemaphoreType.DMA((len(group_sizes(blocks)),)),
            pltpu.SemaphoreType.DMA((3,)),
        ],
        compiler_params=pltpu.CompilerParams(vmem_limit_bytes=FRONT_VMEM),
    )(*[pltpu.with_memory_space_constraint(x, pltpu.HBM) for x in (survive, owner, taps, volts)])

    chips = list(range(stn_count // 2))
    order = [0, 1] + list(range(chan_count - 1, 1, -1))
    out_shape = (RCAP, 2, inputs, stn_count * inputs)

    sequences = []
    for n in chips:
        other = n if n == 0 or (n == chips[-1] and n % 2) else n + 1 if n % 2 else n - 1
        sequences.append((n, other))

    def exchanged(block, distances):
        pairs = [(i, i ^ (2 * distances[i % 2])) for i in range(stn_count)]
        return lax.ppermute(block, "stn", pairs)

    def gathered(block):
        return [block] + [exchanged(block, pair) for pair in sequences[1:]]

    held = jnp.concatenate([pieces[0]] + [swapped(pieces[k], "chan", k) for k in order[1:]], 0)
    slots = held.shape[0]
    near = gathered(held)
    far = [swapped(x, "stn", 1) for x in near]
    ahead, behind = [0, chips[-1]], chips[1:-1]
    lefts, places, result = pl.pallas_call(
        functools.partial(first_kernel, [sequences[n] for n in ahead], order, slot_cap, times),
        out_shape=[
            pltpu.VMEM((slots, 2 * inputs, 2 * lines * pack), jnp.bfloat16),
            pltpu.SMEM((RCAP + 2,), jnp.int32),
            pltpu.VMEM(out_shape, jnp.bfloat16),
        ],
        in_specs=[vmem] * (1 + 2 * len(ahead)),
        out_specs=[vmem, smem, vmem],
        compiler_params=pltpu.CompilerParams(vmem_limit_bytes=BACK_VMEM),
    )(owner, *[near[n] for n in ahead], *[far[n] for n in ahead])
    visibilities, _ = pl.pallas_call(
        functools.partial(back_kernel, [sequences[n] for n in behind], times),
        out_shape=[jax.ShapeDtypeStruct(out_shape, jnp.bfloat16), pltpu.VMEM(out_shape, jnp.bfloat16)],
        in_specs=[smem] + [vmem] * (2 + 2 * len(behind)),
        out_specs=[anywhere, vmem],
        input_output_aliases={2 + 2 * len(behind): 1},
        scratch_shapes=[pltpu.SemaphoreType.DMA((RCAP,))],
        compiler_params=pltpu.CompilerParams(vmem_limit_bytes=BACK_VMEM),
    )(places, *[near[n] for n in behind], *[far[n] for n in behind], lefts, result)
    return visibilities[None]


def solution(mesh):
    return jax.shard_map(
        per_device,
        mesh=mesh,
        in_specs=(P("chan", None, "stn", None), P(), P(), P()),
        out_specs=P("chan", None, None, "stn", None),
        check_vma=False,
    )
```
